32 devices in a mesh: head: 2 (over y), seq: 16 (over z, x, core).
Axes of the slice: x: 2, y: 2, z: 4, core: 2. Of those that a mesh axis runs over, the one named last changes fastest.
Arguments:
- query: bfloat16 [16, 1024, 8192], P('seq', 'head'), may hold values from -40 to 40
- key: bfloat16 [16, 1024, 1024], P('seq', 'head'), may hold values from -4 to 4
- value: bfloat16 [16, 1024, 1024], P('seq', 'head'), may hold values from -6 to 6
- output_gradient: bfloat16 [16, 1024, 8192], P('seq', 'head'), may hold values from -6 to 6
- kv_index: int32 [128, 3], replicated, may hold values from 0 to 127, as said below
- count: int32 [128], replicated, may hold values from 1 to 3, as said below
Outputs:
- attn_out: bfloat16 [16, 1024, 8192], P('seq', 'head')
- grad_query: bfloat16 [16, 1024, 8192], P('seq', 'head')
- key_gradient: bfloat16 [16, 1024, 1024], P('seq', 'head')
- value_gradient: bfloat16 [16, 1024, 1024], P('seq', 'head')
The draws below stay inside these ranges and needn't reach their ends.
Inputs may be any that keep to these rules, and one draw needn't show every extreme that they name: `kv_index`: the first count[i] entries of row i are distinct blocks: i, i-1, down to i-w+1 for some w from 1 to 2, then at most 1 block below i-w+1 that is the last block of some shard (block number ≡ 7 modulo 8). Later entries are arbitrary block numbers. `count`: the number of live entries of each row of kv_index; the last row has 3, the first 1.
All inputs are finite; a program needn't handle non-finite values.
Results may differ from the reference program's by a relative error of at most 0.035.
Values may be sent and summed in bfloat16 or wider, within the bound.
A program may use at most 256 MiB of HBM per device.

```python
import math
import jax
import jax.numpy as jnp
from jax import lax

QUERY_HEADS = 64
KEY_VALUE_HEADS = 8
HEAD_SIZE = 128
BLOCK_TOKENS = 128
WLOC = 2
MAXS = 1
MAXK = 3
BLK_DEV = 8
SHARD_TOKENS = 1024
BLOCK_TOTAL = 128
SEQUENCE_TOKENS = 16384
N_SEQ = 16


def pattern(key):
    key_width = jax.random.fold_in(key, 11)
    key_want = jax.random.fold_in(key, 12)
    key_prio = jax.random.fold_in(key, 13)
    key_fill = jax.random.fold_in(key, 14)
    rows = jnp.arange(BLOCK_TOTAL, dtype=jnp.int32)
    width = jax.random.randint(key_width, (BLOCK_TOTAL,), 1, WLOC + 1, dtype=jnp.int32)
    width = jnp.minimum(width, rows + 1)
    width = width.at[BLOCK_TOTAL - 1].set(WLOC)
    cols = rows[None, :]
    avail = (cols % BLK_DEV == BLK_DEV - 1) & (cols < (rows - width + 1)[:, None])
    navail = jnp.sum(avail.astype(jnp.int32), axis=1)
    want = jax.random.randint(key_want, (BLOCK_TOTAL,), MAXS // 2, MAXS + 1, dtype=jnp.int32)
    want = want.at[BLOCK_TOTAL - 1].set(MAXS)
    nstrided = jnp.minimum(want, navail)
    prio = jax.random.randint(key_prio, (BLOCK_TOTAL, BLOCK_TOTAL), 0, 4096, dtype=jnp.int32) * BLOCK_TOTAL + cols
    prio = jnp.where(avail, prio, -1 - cols)
    unused, picked = lax.top_k(prio, MAXS)
    picked = picked.astype(jnp.int32)
    place = jnp.arange(MAXK, dtype=jnp.int32)[None, :]
    local = rows[:, None] - place
    strided = jnp.take_along_axis(picked, jnp.clip(place - width[:, None], 0, MAXS - 1), axis=1)
    filler = jax.random.randint(key_fill, (BLOCK_TOTAL, MAXK), 0, BLOCK_TOTAL, dtype=jnp.int32)
    table = jnp.where(place < width[:, None], local, jnp.where(place < (width + nstrided)[:, None], strided, filler))
    return (table.astype(jnp.int32), (width + nstrided).astype(jnp.int32))


def draw_kv_index(key, part):
    table, counts = pattern(key)
    return table


def draw_count(key, part):
    table, counts = pattern(key)
    return counts


def fields(key):
    random_key_draw = jax.random.fold_in(key, 21)
    random_query_draw = jax.random.fold_in(key, 22)
    query_group = QUERY_HEADS // KEY_VALUE_HEADS
    key_rows = jax.random.truncated_normal(random_key_draw, -4.0, 4.0, (SEQUENCE_TOKENS, KEY_VALUE_HEADS, HEAD_SIZE), jnp.float32)
    query_rows = jax.random.truncated_normal(random_query_draw, -4.0, 4.0, (SEQUENCE_TOKENS, KEY_VALUE_HEADS, query_group, HEAD_SIZE), jnp.float32)
    return (query_rows.reshape(N_SEQ, SHARD_TOKENS, QUERY_HEADS * HEAD_SIZE), key_rows.reshape(N_SEQ, SHARD_TOKENS, KEY_VALUE_HEADS * HEAD_SIZE))


def draw_query(key, part):
    query_rows, key_rows = fields(key)
    return query_rows.astype(jnp.bfloat16)


def draw_key(key, part):
    query_rows, key_rows = fields(key)
    return key_rows.astype(jnp.bfloat16)


def levels(own_key, shape, shards, smallest, top_value):
    def one(position, parts):
        heights = jax.random.uniform(jax.random.fold_in(jax.random.fold_in(own_key, 6), position), (parts,), jnp.float32, smallest / len(shards), top_value / len(shards))
        return jnp.repeat(jnp.exp(heights), shape[position] // parts).reshape((-1,) + (1,) * (len(shape) - position - 1))

    gain = one(*shards[0])
    for cut in shards[1:]:
        gain = gain * one(*cut)
    return gain


def normal_values(stream_key, dims, scale, limit, cuts=(), kind=jnp.bfloat16):
    factor_of = levels(stream_key, dims, cuts, -0.22, 0.18) if cuts else 1.0
    entries = jax.random.normal(stream_key, dims, jnp.float32) * scale * factor_of
    return jnp.minimum(jnp.maximum(entries, -limit), limit).astype(kind)


def setup_inputs(seed: int = 0) -> dict:
    arg_keys = jax.random.split(jax.random.key(seed), 7)
    return {
        "query": draw_query(jax.random.fold_in(arg_keys[6], 71), 0),
        "key": draw_key(jax.random.fold_in(arg_keys[6], 71), 0),
        "value": normal_values(arg_keys[2], (N_SEQ, SHARD_TOKENS, KEY_VALUE_HEADS * HEAD_SIZE), 1.0, 6.0, ((0, 16), (1, 2))),
        "output_gradient": normal_values(arg_keys[3], (N_SEQ, SHARD_TOKENS, QUERY_HEADS * HEAD_SIZE), 1.0, 6.0, ((0, 16), (1, 2))),
        "kv_index": draw_kv_index(jax.random.fold_in(arg_keys[6], 71), 0),
        "count": draw_count(jax.random.fold_in(arg_keys[6], 71), 0),
    }


def reference(query, key, value, output_gradient, kv_index, count):
    query_group = QUERY_HEADS // KEY_VALUE_HEADS
    scale = 1.0 / math.sqrt(HEAD_SIZE)
    query_rows_full = query.reshape(BLOCK_TOTAL, BLOCK_TOKENS, KEY_VALUE_HEADS, query_group, HEAD_SIZE)
    gradient_output_rows = output_gradient.reshape(BLOCK_TOTAL, BLOCK_TOKENS, KEY_VALUE_HEADS, query_group, HEAD_SIZE)
    key_rows_full = key.reshape(BLOCK_TOTAL, BLOCK_TOKENS, KEY_VALUE_HEADS, HEAD_SIZE)
    value_rows_full = value.reshape(BLOCK_TOTAL, BLOCK_TOKENS, KEY_VALUE_HEADS, HEAD_SIZE)
    place = jnp.arange(MAXK, dtype=jnp.int32)
    tokens = jnp.arange(BLOCK_TOKENS, dtype=jnp.int32)
    tails = (jnp.arange(N_SEQ, dtype=jnp.int32) * BLK_DEV + BLK_DEV - 1).astype(jnp.int32)

    def row_step(carry, row):
        key_gradient_total, value_gradient_total, far_k, far_v = carry
        shard = (row // BLK_DEV).astype(jnp.int32)
        ids = kv_index[row]
        live = place < count[row]
        index = jnp.where(live, ids, 0).astype(jnp.int32)
        owner = (index // BLK_DEV).astype(jnp.int32)
        inside = live & (owner == shard)
        outside = live & (owner != shard)
        qb = query_rows_full[row].astype(jnp.float32)
        gb = gradient_output_rows[row]
        kb = key_rows_full[index].astype(jnp.float32)
        vb = value_rows_full[index].astype(jnp.float32)
        allowed = live[None, :, None] & ((ids[None, :, None] != row) | (tokens[None, None, :] <= tokens[:, None, None]))
        score = jnp.einsum('acgd,mncd->cgamn', qb, kb) * scale
        score = jnp.where(allowed[None, None], score, -1e+30)
        top = lax.optimization_barrier(jnp.max(score, axis=(3, 4), keepdims=True))
        expo = jnp.exp(score - top)
        prob = expo / lax.optimization_barrier(jnp.sum(expo, axis=(3, 4), keepdims=True))
        prob_b = prob.astype(jnp.bfloat16)
        out_b = jnp.einsum('cgamn,mncd->acgd', prob_b.astype(jnp.float32), vb).astype(jnp.bfloat16)
        delta = lax.optimization_barrier(jnp.sum(gb.astype(jnp.float32) * out_b.astype(jnp.float32), axis=-1))
        delta = jnp.transpose(delta, (1, 2, 0))[:, :, :, None, None]
        dprob = jnp.einsum('acgd,mncd->cgamn', gb.astype(jnp.float32), vb)
        dscore = (prob * (dprob - delta)).astype(jnp.bfloat16).astype(jnp.float32)
        dq = (jnp.einsum('cgamn,mncd->acgd', dscore, kb) * scale).astype(jnp.bfloat16)
        dv_slots = jnp.einsum('cgamn,acgd->mncd', prob_b.astype(jnp.float32), gb.astype(jnp.float32))
        dk_slots = jnp.einsum('cgamn,acgd->mncd', dscore, qb) * scale
        mask_in = inside[:, None, None, None]
        mask_out = outside[:, None, None, None]
        key_gradient_total = key_gradient_total.at[index].add(jnp.where(mask_in, dk_slots, 0.0))
        value_gradient_total = value_gradient_total.at[index].add(jnp.where(mask_in, dv_slots, 0.0))
        far_k = far_k.at[owner].add(jnp.where(mask_out, dk_slots, 0.0))
        far_v = far_v.at[owner].add(jnp.where(mask_out, dv_slots, 0.0))
        return ((key_gradient_total, value_gradient_total, far_k, far_v), (out_b, dq))

    def shard_step(carry, shard):
        key_gradient_total, value_gradient_total = carry
        blank_slots = jnp.zeros((N_SEQ, BLOCK_TOKENS, KEY_VALUE_HEADS, HEAD_SIZE), jnp.float32)
        rows = (shard * BLK_DEV + jnp.arange(BLK_DEV, dtype=jnp.int32)).astype(jnp.int32)
        (key_gradient_total, value_gradient_total, far_k, far_v), (outs, dqs) = lax.scan(row_step, (key_gradient_total, value_gradient_total, blank_slots, blank_slots), rows)
        far_k = lax.optimization_barrier(far_k.astype(jnp.bfloat16)).astype(jnp.float32)
        far_v = lax.optimization_barrier(far_v.astype(jnp.bfloat16)).astype(jnp.float32)
        key_gradient_total = key_gradient_total.at[tails].add(far_k)
        value_gradient_total = value_gradient_total.at[tails].add(far_v)
        return ((key_gradient_total, value_gradient_total), (outs, dqs))
    block_offset = (jnp.zeros((BLOCK_TOTAL, BLOCK_TOKENS, KEY_VALUE_HEADS, HEAD_SIZE), jnp.float32), jnp.zeros((BLOCK_TOTAL, BLOCK_TOKENS, KEY_VALUE_HEADS, HEAD_SIZE), jnp.float32))
    (key_gradient_total, value_gradient_total), (outs, dqs) = lax.scan(shard_step, block_offset, jnp.arange(N_SEQ, dtype=jnp.int32))
    attn_out = outs.reshape(N_SEQ, SHARD_TOKENS, QUERY_HEADS * HEAD_SIZE)
    grad_query = dqs.reshape(N_SEQ, SHARD_TOKENS, QUERY_HEADS * HEAD_SIZE)
    key_gradient = key_gradient_total.astype(jnp.bfloat16).reshape(N_SEQ, SHARD_TOKENS, KEY_VALUE_HEADS * HEAD_SIZE)
    value_gradient = value_gradient_total.astype(jnp.bfloat16).reshape(N_SEQ, SHARD_TOKENS, KEY_VALUE_HEADS * HEAD_SIZE)
    return (attn_out, grad_query, key_gradient, value_gradient)
```

```python
import functools
import math

import jax
import jax.numpy as jnp
from jax import lax
from jax.experimental import pallas as pl
from jax.experimental.pallas import tpu as pltpu
from jax.sharding import PartitionSpec as P

HEAD = 128
TOK = 128
MAXK = 3
DEAD = -1e30
CHUNKS = 1
SPLIT = 4


def attend(
    nb, nseq, query_group,
    meta,
    q_ref, g_ref, k_ref, v_ref, near_ref, tail_ref, *rest,
):
    out_ref, dq_ref, dk_ref, dv_ref, dnear_ref, dtail_ref, x_ref, pd_ref, far_ref = rest[-9:]
    f32, bf16 = jnp.float32, jnp.bfloat16
    scale = 1.0 / math.sqrt(HEAD)
    factor = scale * math.log2(math.e)
    zero = jnp.zeros((TOK, HEAD), bf16)
    causal = (
        lax.broadcasted_iota(jnp.int32, (TOK, TOK), 0)
        <= lax.broadcasted_iota(jnp.int32, (TOK, TOK), 1)
    )
    bias = jnp.where(causal, 0.0, DEAD).astype(f32)
    bias = jnp.concatenate([bias] * SPLIT, axis=1)
    prev_is_tail = meta[3 * nb] > 0
    prev_slot = pl.multiple_of(meta[3 * nb + 1] * TOK, TOK)
    dtail_ref[...] = jnp.zeros_like(dtail_ref)
    dnear_ref[...] = jnp.zeros_like(dnear_ref)

    for r in range(nb):
        rows = slice(r * TOK, (r + 1) * TOK)
        live = [None, meta[3 * r] > 0, meta[3 * r + 1] > 0]
        slot = pl.multiple_of(meta[3 * r + 2] * TOK, TOK)
        kv = [(k_ref[rows, :], v_ref[rows, :])]
        if r:
            before = slice((r - 1) * TOK, r * TOK)
            kv.append((k_ref[before, :], v_ref[before, :]))
        else:
            tail = tail_ref[pl.ds(prev_slot, TOK), :]
            pick = jnp.where(prev_is_tail, tail.astype(f32), near_ref[...].astype(f32)).astype(bf16)
            kv.append((pick[:, :HEAD], pick[:, HEAD:]))
        tail = tail_ref[pl.ds(slot, TOK), :]
        kv.append((tail[:, :HEAD], tail[:, HEAD:]))
        a = jnp.concatenate(
            [
                part
                for k, v in kv
                for part in (
                    jnp.concatenate([k, zero], axis=1),
                    jnp.concatenate([zero, v], axis=1),
                )
            ],
            axis=0,
        )
        b = jnp.concatenate(
            [
                jnp.concatenate(
                    [part for k, v in kv for part in (v.T, zero)], axis=1
                ),
                jnp.concatenate(
                    [part for k, v in kv for part in (zero, k.T)], axis=1
                ),
            ],
            axis=0,
        )
        for c in range(query_group // SPLIT):
            span = SPLIT * TOK
            at = slice(c * span, (c + 1) * span)
            for h in range(SPLIT):
                lanes = slice((c * SPLIT + h) * HEAD, (c * SPLIT + h + 1) * HEAD)
                there = slice((c * SPLIT + h) * TOK, (c * SPLIT + h + 1) * TOK)
                x_ref[there, :HEAD] = q_ref[rows, lanes]
                x_ref[there, HEAD:] = g_ref[rows, lanes]
            st = lax.dot_general(
                a, x_ref[at, :], (((1,), (1,)), ((), ())), preferred_element_type=f32
            )
            s = [st[2 * j * TOK : (2 * j + 1) * TOK] for j in range(MAXK)]
            dp = [st[(2 * j + 1) * TOK : (2 * j + 2) * TOK] for j in range(MAXK)]
            s[0] = s[0] + bias
            tops = [jnp.max(x, axis=0, keepdims=True) for x in s]
            top = tops[0]
            for j in (1, 2):
                top = jnp.maximum(top, jnp.where(live[j], tops[j], DEAD))
            p = []
            for j in range(MAXK):
                base = top if j == 0 else jnp.where(live[j], top, -DEAD)
                p.append(jnp.exp2((s[j] - base) * factor))
            total = sum(jnp.sum(x, axis=0, keepdims=True) for x in p)
            inv = 1.0 / total
            delta = sum(jnp.sum(x * y, axis=0, keepdims=True) for x, y in zip(p, dp)) * inv
            for j in range(MAXK):
                prob = p[j] * inv
                pd_ref[2 * j * TOK : (2 * j + 1) * TOK, at] = prob.astype(bf16)
                pd_ref[(2 * j + 1) * TOK : (2 * j + 2) * TOK, at] = (
                    prob * (dp[j] - delta)
                ).astype(bf16)
            ot = jnp.dot(b, pd_ref[:, at], preferred_element_type=f32)
            for h in range(SPLIT):
                lanes = slice((c * SPLIT + h) * HEAD, (c * SPLIT + h + 1) * HEAD)
                piece = ot[:, h * TOK : (h + 1) * TOK]
                out_ref[rows, lanes] = piece[:HEAD].T.astype(bf16)
                dq_ref[rows, lanes] = (piece[HEAD:].T * scale).astype(bf16)
        dkv = jnp.dot(pd_ref[...], x_ref[...], preferred_element_type=f32)

        def grads(j):
            return (
                dkv[(2 * j + 1) * TOK : (2 * j + 2) * TOK, :HEAD] * scale,
                dkv[2 * j * TOK : (2 * j + 1) * TOK, HEAD:],
            )

        dk, dv = grads(0)
        dk_ref[rows, :] = dk
        dv_ref[rows, :] = dv
        dk, dv = grads(1)
        if r:
            dk_ref[before, :] += dk
            dv_ref[before, :] += dv
        else:
            far_ref[nb, :, :HEAD] = dk
            far_ref[nb, :, HEAD:] = dv
        dk, dv = grads(2)
        far_ref[r, :, :HEAD] = dk
        far_ref[r, :, HEAD:] = dv

    first = far_ref[nb]
    first_far = jnp.logical_and(prev_is_tail, meta[0] > 0)

    @pl.when(jnp.logical_not(prev_is_tail))
    def _():
        dnear_ref[...] = first.astype(bf16)

    @pl.when(first_far)
    def _():
        dtail_ref[pl.ds(prev_slot, TOK), :] = first.astype(bf16)

    for r in range(nb):
        @pl.when(meta[3 * r + 1] > 0)
        def _(r=r):
            mine = meta[3 * r + 2]
            sum_ = far_ref[r]
            same = jnp.logical_and(first_far, meta[3 * nb + 1] == mine)
            sum_ = sum_ + jnp.where(same, far_ref[nb], 0.0)
            for e in range(r):
                same = jnp.logical_and(meta[3 * e + 1] > 0, meta[3 * e + 2] == mine)
                sum_ = sum_ + jnp.where(same, far_ref[e], 0.0)
            dtail_ref[pl.ds(pl.multiple_of(mine * TOK, TOK), TOK), :] = sum_.astype(bf16)


def call(nb, nseq, width, first, groups, query_group, meta, q, g, k, v, near, tails, earlier):
    rows = nb * TOK
    wide = query_group * HEAD
    width_kv = k.shape[1]

    def at(i, meta):
        return (0, i)

    def global_at(i, meta):
        return (0, first + i)

    big = pl.BlockSpec((rows, wide), global_at)
    own = pl.BlockSpec((rows, HEAD), global_at)
    in_specs = [
        big, big, own, own,
        pl.BlockSpec((TOK, 2 * HEAD), at),
        pl.BlockSpec((nseq * TOK, 2 * HEAD), at),
    ]
    operands = [q, g, k, v, near, tails]
    aliases = {}
    for i, e in enumerate(earlier):
        aliases[1 + len(operands)] = i
        operands.append(e)
        in_specs.append(pl.BlockSpec(memory_space=pl.ANY))
    bf16, f32 = jnp.bfloat16, jnp.float32
    sds = jax.ShapeDtypeStruct
    flops = 2 * rows * wide * MAXK * TOK * 6 * groups
    return pl.pallas_call(
        functools.partial(attend, nb, nseq, query_group),
        out_shape=(
            sds((rows, width), bf16), sds((rows, width), bf16),
            sds((rows, width_kv), f32), sds((rows, width_kv), f32),
            sds((TOK, groups * 2 * HEAD), bf16),
            sds((nseq * TOK, groups * 2 * HEAD), bf16),
        ),
        grid_spec=pltpu.PrefetchScalarGridSpec(
            num_scalar_prefetch=1,
            grid=(groups,),
            in_specs=in_specs,
            out_specs=[
                big, big, own, own,
                pl.BlockSpec((TOK, 2 * HEAD), at),
                pl.BlockSpec((nseq * TOK, 2 * HEAD), at),
            ],
            scratch_shapes=[
                pltpu.VMEM((query_group * TOK, 2 * HEAD), bf16),
                pltpu.VMEM((2 * MAXK * TOK, query_group * TOK), bf16),
                pltpu.VMEM((nb + 1, TOK, 2 * HEAD), f32),
            ],
        ),
        input_output_aliases=aliases,
        compiler_params=pltpu.CompilerParams(
            dimension_semantics=("arbitrary",), vmem_limit_bytes=48 * 1024 * 1024
        ),
        cost_estimate=pl.CostEstimate(
            flops=flops, bytes_accessed=4 * 2 * rows * wide * groups, transcendentals=0
        ),
        name="attend",
    )(meta, *operands)


def shards(query, key, value, output_gradient, kv_index, count):
    nseq, nhead = lax.axis_size("seq"), lax.axis_size("head")
    shard, part = lax.axis_index("seq"), lax.axis_index("head")
    rows, width = query.shape[1:]
    width_kv = key.shape[2]
    nb = rows // TOK
    ngroup = width_kv // HEAD
    query_group = width // width_kv
    blocks = nb * nhead
    row0 = shard * blocks + part * nb
    ids = lax.dynamic_slice_in_dim(kv_index, row0, nb, 0)
    n = lax.dynamic_slice_in_dim(count, row0, nb, 0)
    row = row0 + jnp.arange(nb, dtype=jnp.int32)
    prev = (n >= 2) & (ids[:, 1] == row - 1)
    strided = (n == 3) | ((n == 2) & ~prev)
    owner = jnp.where(n == 3, ids[:, 2], ids[:, 1]) // blocks
    owner = jnp.where(strided, owner, 0)
    per_row = jnp.stack([prev.astype(jnp.int32), strided.astype(jnp.int32), owner], axis=1)
    ends = jnp.stack([(part == 0).astype(jnp.int32), jnp.maximum(shard - 1, 0)])
    meta = jnp.concatenate([per_row.reshape(-1), ends]).astype(jnp.int32)

    q, g, k, v = query[0], output_gradient[0], key[0], value[0]
    last = jnp.stack(
        [k[rows - TOK :].reshape(TOK, ngroup, HEAD), v[rows - TOK :].reshape(TOK, ngroup, HEAD)],
        axis=2,
    ).reshape(TOK, 2 * width_kv)
    step = ngroup // CHUNKS
    cols = step * 2 * HEAD
    up = [(i, i + 1) for i in range(nhead - 1)]
    pair = [(0, 1), (1, 0)]
    if nhead == 2:
        near = lax.ppermute(last, "head", pair)
        tail = jnp.where(part == 1, last, near)
    else:
        near = lax.ppermute(last, "head", up)
        tail = lax.all_gather(last, "head", axis=0)[nhead - 1]
    gathered = [
        lax.all_gather(tail[:, c * cols : (c + 1) * cols], "seq", axis=0, tiled=True)
        for c in range(CHUNKS)
    ]
    earlier = ()
    tail_grads, near_grads = [], []
    for c in range(CHUNKS):
        *earlier, near_grad, tail_grad = call(
            nb, nseq, width, c * step, step, query_group, meta, q, g, k, v,
            near[:, c * cols : (c + 1) * cols], gathered[c], earlier,
        )
        near_grads.append(near_grad)
        tail_grads.append(
            lax.psum_scatter(tail_grad, "seq", scatter_dimension=0, tiled=True)
        )
    attn, dquery, dkey, dvalue = earlier
    near_grad = jnp.concatenate(near_grads, axis=1)
    tail_grad = jnp.concatenate(tail_grads, axis=1)
    if nhead == 2:
        other = lax.ppermute(jnp.where(part == 0, tail_grad, near_grad), "head", pair)
        add = other.astype(jnp.float32) + jnp.where(part == 1, tail_grad.astype(jnp.float32), 0.0)
    else:
        total = lax.psum(tail_grad, "head").astype(jnp.float32)
        other = lax.ppermute(near_grad, "head", [(j, i) for i, j in up])
        add = other.astype(jnp.float32) + jnp.where(part == nhead - 1, total, 0.0)
    add = add.reshape(TOK, ngroup, 2, HEAD)
    dkey = dkey.at[rows - TOK :].add(add[:, :, 0].reshape(TOK, width_kv))
    dvalue = dvalue.at[rows - TOK :].add(add[:, :, 1].reshape(TOK, width_kv))
    return (
        attn[None], dquery[None],
        dkey.astype(jnp.bfloat16)[None], dvalue.astype(jnp.bfloat16)[None],
    )


def solution(mesh):
    spec = P("seq", "head", None)
    return jax.shard_map(
        shards,
        mesh=mesh,
        in_specs=(spec,) * 4 + (P(), P()),
        out_specs=(spec,) * 4,
        check_vma=False,
    )
```

```python
import functools
import math

import jax
import jax.numpy as jnp
from jax import lax
from jax.experimental import pallas as pl
from jax.experimental.pallas import tpu as pltpu
from jax.sharding import PartitionSpec as P

HEAD = 128
TOK = 128
MAXK = 3
DEAD = -1e30
CHUNKS = 1
SPLIT = 4


def attend(
    nb, nseq, query_group,
    meta,
    q_ref, g_ref, k_ref, v_ref, near_ref, tail_ref, *rest,
):
    out_ref, dq_ref, dk_ref, dv_ref, dnear_ref, dtail_ref, x_ref, pd_ref, far_ref = rest[-9:]
    f32, bf16 = jnp.float32, jnp.bfloat16
    scale = 1.0 / math.sqrt(HEAD)
    factor = scale * math.log2(math.e)
    zero = jnp.zeros((TOK, HEAD), bf16)
    causal = (
        lax.broadcasted_iota(jnp.int32, (TOK, TOK), 0)
        <= lax.broadcasted_iota(jnp.int32, (TOK, TOK), 1)
    )
    bias = jnp.where(causal, 0.0, DEAD).astype(f32)
    bias = jnp.concatenate([bias] * SPLIT, axis=1)
    prev_is_tail = meta[3 * nb] > 0
    prev_slot = pl.multiple_of(meta[3 * nb + 1] * TOK, TOK)
    dtail_ref[...] = jnp.zeros_like(dtail_ref)
    dnear_ref[...] = jnp.zeros_like(dnear_ref)

    for r in range(nb):
        rows = slice(r * TOK, (r + 1) * TOK)
        live = [None, meta[3 * r] > 0, meta[3 * r + 1] > 0]
        slot = pl.multiple_of(meta[3 * r + 2] * TOK, TOK)
        kv = [(k_ref[rows, :], v_ref[rows, :])]
        if r:
            before = slice((r - 1) * TOK, r * TOK)
            kv.append((k_ref[before, :], v_ref[before, :]))
        else:
            tail = tail_ref[pl.ds(prev_slot, TOK), :]
            pick = jnp.where(prev_is_tail, tail.astype(f32), near_ref[...].astype(f32)).astype(bf16)
            kv.append((pick[:, :HEAD], pick[:, HEAD:]))
        tail = tail_ref[pl.ds(slot, TOK), :]
        kv.append((tail[:, :HEAD], tail[:, HEAD:]))
        a = jnp.concatenate(
            [
                part
                for k, v in kv
                for part in (
                    jnp.concatenate([k, zero], axis=1),
                    jnp.concatenate([zero, v], axis=1),
                )
            ],
            axis=0,
        )
        b = jnp.concatenate(
            [
                jnp.concatenate(
                    [part for k, v in kv for part in (v.T, zero)], axis=1
                ),
                jnp.concatenate(
                    [part for k, v in kv for part in (zero, k.T)], axis=1
                ),
            ],
            axis=0,
        )
        for c in range(query_group // SPLIT):
            span = SPLIT * TOK
            at = slice(c * span, (c + 1) * span)
            for h in range(SPLIT):
                lanes = slice((c * SPLIT + h) * HEAD, (c * SPLIT + h + 1) * HEAD)
                there = slice((c * SPLIT + h) * TOK, (c * SPLIT + h + 1) * TOK)
                x_ref[there, :HEAD] = q_ref[rows, lanes]
                x_ref[there, HEAD:] = g_ref[rows, lanes]
            st = lax.dot_general(
                a, x_ref[at, :], (((1,), (1,)), ((), ())), preferred_element_type=f32
            )
            s = [st[2 * j * TOK : (2 * j + 1) * TOK] for j in range(MAXK)]
            dp = [st[(2 * j + 1) * TOK : (2 * j + 2) * TOK] for j in range(MAXK)]
            s[0] = s[0] + bias
            tops = [jnp.max(x, axis=0, keepdims=True) for x in s]
            top = tops[0]
            for j in (1, 2):
                top = jnp.maximum(top, jnp.where(live[j], tops[j], DEAD))
            p = []
            for j in range(MAXK):
                base = top if j == 0 else jnp.where(live[j], top, -DEAD)
                p.append(jnp.exp2((s[j] - base) * factor))
            total = sum(jnp.sum(x, axis=0, keepdims=True) for x in p)
            inv = 1.0 / total
            delta = sum(jnp.sum(x * y, axis=0, keepdims=True) for x, y in zip(p, dp)) * inv
            for j in range(MAXK):
                prob = p[j] * inv
                pd_ref[2 * j * TOK : (2 * j + 1) * TOK, at] = prob.astype(bf16)
                pd_ref[(2 * j + 1) * TOK : (2 * j + 2) * TOK, at] = (
                    prob * (dp[j] - delta)
                ).astype(bf16)
            ot = jnp.dot(b, pd_ref[:, at], preferred_element_type=f32)
            for h in range(SPLIT):
                lanes = slice((c * SPLIT + h) * HEAD, (c * SPLIT + h + 1) * HEAD)
                piece = ot[:, h * TOK : (h + 1) * TOK]
                out_ref[rows, lanes] = piece[:HEAD].T.astype(bf16)
                dq_ref[rows, lanes] = (piece[HEAD:].T * scale).astype(bf16)
        dkv = jnp.dot(pd_ref[...], x_ref[...], preferred_element_type=f32)

        def grads(j):
            return (
                dkv[(2 * j + 1) * TOK : (2 * j + 2) * TOK, :HEAD] * scale,
                dkv[2 * j * TOK : (2 * j + 1) * TOK, HEAD:],
            )

        dk, dv = grads(0)
        dk_ref[rows, :] = dk
        dv_ref[rows, :] = dv
        dk, dv = grads(1)
        if r:
            dk_ref[before, :] += dk
            dv_ref[before, :] += dv
        else:
            far_ref[nb, :, :HEAD] = dk
            far_ref[nb, :, HEAD:] = dv
        dk, dv = grads(2)
        far_ref[r, :, :HEAD] = dk
        far_ref[r, :, HEAD:] = dv

    first = far_ref[nb]
    first_far = jnp.logical_and(prev_is_tail, meta[0] > 0)

    @pl.when(jnp.logical_not(prev_is_tail))
    def _():
        dnear_ref[...] = first.astype(bf16)

    @pl.when(first_far)
    def _():
        dtail_ref[pl.ds(prev_slot, TOK), :] = first.astype(bf16)

    for r in range(nb):
        @pl.when(meta[3 * r + 1] > 0)
        def _(r=r):
            mine = meta[3 * r + 2]
            sum_ = far_ref[r]
            same = jnp.logical_and(first_far, meta[3 * nb + 1] == mine)
            sum_ = sum_ + jnp.where(same, far_ref[nb], 0.0)
            for e in range(r):
                same = jnp.logical_and(meta[3 * e + 1] > 0, meta[3 * e + 2] == mine)
                sum_ = sum_ + jnp.where(same, far_ref[e], 0.0)
            dtail_ref[pl.ds(pl.multiple_of(mine * TOK, TOK), TOK), :] = sum_.astype(bf16)


def call(nb, nseq, width, first, groups, query_group, meta, q, g, k, v, near, tails, earlier):
    rows = nb * TOK
    wide = query_group * HEAD
    width_kv = k.shape[1]

    def at(i, meta):
        return (0, i)

    def global_at(i, meta):
        return (0, first + i)

    big = pl.BlockSpec((rows, wide), global_at)
    own = pl.BlockSpec((rows, HEAD), global_at)
    in_specs = [
        big, big, own, own,
        pl.BlockSpec((TOK, 2 * HEAD), at),
        pl.BlockSpec((nseq * TOK, 2 * HEAD), at),
    ]
    operands = [q, g, k, v, near, tails]
    aliases = {}
    for i, e in enumerate(earlier):
        aliases[1 + len(operands)] = i
        operands.append(e)
        in_specs.append(pl.BlockSpec(memory_space=pl.ANY))
    bf16, f32 = jnp.bfloat16, jnp.float32
    sds = jax.ShapeDtypeStruct
    flops = 2 * rows * wide * MAXK * TOK * 6 * groups
    return pl.pallas_call(
        functools.partial(attend, nb, nseq, query_group),
        out_shape=(
            sds((rows, width), bf16), sds((rows, width), bf16),
            sds((rows, width_kv), f32), sds((rows, width_kv), f32),
            sds((TOK, groups * 2 * HEAD), bf16),
            sds((nseq * TOK, groups * 2 * HEAD), bf16),
        ),
        grid_spec=pltpu.PrefetchScalarGridSpec(
            num_scalar_prefetch=1,
            grid=(groups,),
            in_specs=in_specs,
            out_specs=[
                big, big, own, own,
                pl.BlockSpec((TOK, 2 * HEAD), at),
                pl.BlockSpec((nseq * TOK, 2 * HEAD), at),
            ],
            scratch_shapes=[
                pltpu.VMEM((query_group * TOK, 2 * HEAD), bf16),
                pltpu.VMEM((2 * MAXK * TOK, query_group * TOK), bf16),
                pltpu.VMEM((nb + 1, TOK, 2 * HEAD), f32),
            ],
        ),
        input_output_aliases=aliases,
        compiler_params=pltpu.CompilerParams(
            dimension_semantics=("arbitrary",), vmem_limit_bytes=48 * 1024 * 1024
        ),
        cost_estimate=pl.CostEstimate(
            flops=flops, bytes_accessed=4 * 2 * rows * wide * groups, transcendentals=0
        ),
        name="attend",
    )(meta, *operands)


PIECES = 2


def ring_place(n):
    across = n // 8
    me = lax.axis_index("seq")
    x, z = me // 2 % across, me // (2 * across)
    place = (x * 4 + z + (x % 2) * (3 - 2 * z)) * 2 + me % 2

    def index(p):
        p = (p + n) % n
        x, z = p // 8, p // 2 % 4
        z = z + (x % 2) * (3 - 2 * z)
        return z * (2 * across) + x * 2 + p % 2

    return me, place, index


def greet(left, right):
    barrier = pltpu.get_barrier_semaphore()
    for neighbour in (left, right):
        pl.semaphore_signal(
            barrier, inc=1, device_id={"seq": neighbour}, device_id_type=pl.DeviceIdType.MESH
        )
    pl.semaphore_wait(barrier, 2)


LANES = [(way, piece) for piece in range(PIECES) for way in range(2)]


def gather_ring(n, half, tail_ref, out_ref, send_sem, recv_sem, own_sem):
    me, place, index = ring_place(n)
    right, left = index(place + 1), index(place - 1)
    size = TOK // PIECES
    greet(left, right)

    def window(t, way, piece):
        owner = index(place - t) if way == 0 else index(place + t)
        start = pl.multiple_of(owner * TOK + piece * size, size)
        return out_ref.at[pl.ds(start, size), pl.ds(way * half, half)]

    def copy(t, sem, way, piece, src=None):
        there = window(t, way, piece)
        return pltpu.make_async_remote_copy(
            src_ref=there if src is None else src,
            dst_ref=there,
            send_sem=send_sem.at[way, piece, sem],
            recv_sem=recv_sem.at[way, piece, sem],
            device_id={"seq": right if way == 0 else left},
            device_id_type=pl.DeviceIdType.MESH,
        )

    for way, piece in LANES:
        src = tail_ref.at[pl.ds(piece * size, size), pl.ds(way * half, half)]
        copy(0, 0, way, piece, src).start()
    own = pltpu.make_async_copy(
        tail_ref, out_ref.at[pl.ds(pl.multiple_of(me * TOK, TOK), TOK), :], own_sem
    )
    own.start()

    def step(t, carry):
        for way, piece in LANES:
            copy(t, t - 1, way, piece).wait_recv()
            copy(t, t, way, piece).start()
        return carry

    lax.fori_loop(1, n - 1, step, 0)
    for way, piece in LANES:
        copy(n - 1, n - 2, way, piece).wait_recv()
    own.wait()

    def finish(t, carry):
        for way, piece in LANES:
            copy(t, t, way, piece).wait_send()
        return carry

    lax.fori_loop(0, n - 1, finish, 0)


def reduce_ring(n, half, term_ref, sum_ref, slots, send_sem, recv_sem):
    me, place, index = ring_place(n)
    right, left = index(place + 1), index(place - 1)
    size = TOK // PIECES
    greet(left, right)

    def term(t, way, piece):
        owner = index(place - 1 - t) if way == 0 else index(place + 1 + t)
        start = pl.multiple_of(owner * TOK + piece * size, size)
        return term_ref.at[pl.ds(start, size), pl.ds(way * half, half)]

    def slot(t, way, piece):
        return slots.at[t, way, pl.ds(piece * size, size), :]

    def copy(t, way, piece, src):
        return pltpu.make_async_remote_copy(
            src_ref=src,
            dst_ref=slot(t, way, piece),
            send_sem=send_sem.at[way, piece, t],
            recv_sem=recv_sem.at[way, piece, t],
            device_id={"seq": right if way == 0 else left},
            device_id_type=pl.DeviceIdType.MESH,
        )

    for way, piece in LANES:
        copy(0, way, piece, term(0, way, piece)).start()

    def total(t, way, piece):
        held = slot(t - 1, way, piece)
        copy(t - 1, way, piece, held).wait_recv()
        return held[...].astype(jnp.float32) + term(t, way, piece)[...].astype(jnp.float32)

    def step(t, carry):
        for way, piece in LANES:
            value = total(t, way, piece)
            held = slot(t - 1, way, piece)
            held[...] = value.astype(jnp.bfloat16)
            copy(t, way, piece, held).start()
        return carry

    lax.fori_loop(1, n - 1, step, 0)
    for way, piece in LANES:
        sum_ref[piece * size : (piece + 1) * size, way * half : (way + 1) * half] = total(
            n - 1, way, piece
        ).astype(jnp.bfloat16)

    def finish(t, carry):
        for way, piece in LANES:
            copy(t, way, piece, slot(t, way, piece)).wait_send()
        return carry

    lax.fori_loop(0, n - 1, finish, 0)


def gather(tail, n):
    half = tail.shape[1] // 2
    sems = pltpu.SemaphoreType.DMA((2, PIECES, n - 1))
    return pl.pallas_call(
        functools.partial(gather_ring, n, half),
        out_shape=jax.ShapeDtypeStruct((n * TOK, 2 * half), tail.dtype),
        in_specs=[pl.BlockSpec(memory_space=pl.ANY)],
        out_specs=pl.BlockSpec(memory_space=pl.ANY),
        scratch_shapes=[sems, sems, pltpu.SemaphoreType.DMA],
        compiler_params=pltpu.CompilerParams(collective_id=0, has_side_effects=True),
        name="gather_ring",
    )(tail)


def reduce_scatter(terms, n):
    half = terms.shape[1] // 2
    sems = pltpu.SemaphoreType.DMA((2, PIECES, n - 1))
    return pl.pallas_call(
        functools.partial(reduce_ring, n, half),
        out_shape=jax.ShapeDtypeStruct((TOK, 2 * half), terms.dtype),
        in_specs=[pl.BlockSpec(memory_space=pltpu.VMEM)],
        out_specs=pl.BlockSpec(memory_space=pltpu.VMEM),
        scratch_shapes=[pltpu.VMEM((n - 1, 2, TOK, half), terms.dtype), sems, sems],
        compiler_params=pltpu.CompilerParams(
            collective_id=1, has_side_effects=True, vmem_limit_bytes=48 * 1024 * 1024
        ),
        name="reduce_ring",
    )(terms)


def shards(query, key, value, output_gradient, kv_index, count):
    nseq, nhead = lax.axis_size("seq"), lax.axis_size("head")
    shard, part = lax.axis_index("seq"), lax.axis_index("head")
    rows, width = query.shape[1:]
    width_kv = key.shape[2]
    nb = rows // TOK
    ngroup = width_kv // HEAD
    query_group = width // width_kv
    blocks = nb * nhead
    row0 = shard * blocks + part * nb
    ids = lax.dynamic_slice_in_dim(kv_index, row0, nb, 0)
    n = lax.dynamic_slice_in_dim(count, row0, nb, 0)
    row = row0 + jnp.arange(nb, dtype=jnp.int32)
    prev = (n >= 2) & (ids[:, 1] == row - 1)
    strided = (n == 3) | ((n == 2) & ~prev)
    owner = jnp.where(n == 3, ids[:, 2], ids[:, 1]) // blocks
    owner = jnp.where(strided, owner, 0)
    per_row = jnp.stack([prev.astype(jnp.int32), strided.astype(jnp.int32), owner], axis=1)
    ends = jnp.stack([(part == 0).astype(jnp.int32), jnp.maximum(shard - 1, 0)])
    meta = jnp.concatenate([per_row.reshape(-1), ends]).astype(jnp.int32)

    q, g, k, v = query[0], output_gradient[0], key[0], value[0]
    last = jnp.stack(
        [k[rows - TOK :].reshape(TOK, ngroup, HEAD), v[rows - TOK :].reshape(TOK, ngroup, HEAD)],
        axis=2,
    ).reshape(TOK, 2 * width_kv)
    step = ngroup // CHUNKS
    cols = step * 2 * HEAD
    up = [(i, i + 1) for i in range(nhead - 1)]
    pair = [(0, 1), (1, 0)]
    if nhead == 2:
        near = lax.ppermute(last, "head", pair)
        tail = jnp.where(part == 1, last, near)
    else:
        near = lax.ppermute(last, "head", up)
        tail = lax.all_gather(last, "head", axis=0)[nhead - 1]
    gathered = [
        gather(tail[:, c * cols : (c + 1) * cols], nseq)
        for c in range(CHUNKS)
    ]
    earlier = ()
    tail_grads, near_grads = [], []
    for c in range(CHUNKS):
        *earlier, near_grad, tail_grad = call(
            nb, nseq, width, c * step, step, query_group, meta, q, g, k, v,
            near[:, c * cols : (c + 1) * cols], gathered[c], earlier,
        )
        near_grads.append(near_grad)
        tail_grads.append(reduce_scatter(tail_grad, nseq))
    attn, dquery, dkey, dvalue = earlier
    near_grad = jnp.concatenate(near_grads, axis=1)
    tail_grad = jnp.concatenate(tail_grads, axis=1)
    if nhead == 2:
        other = lax.ppermute(jnp.where(part == 0, tail_grad, near_grad), "head", pair)
        add = other.astype(jnp.float32) + jnp.where(part == 1, tail_grad.astype(jnp.float32), 0.0)
    else:
        total = lax.psum(tail_grad, "head").astype(jnp.float32)
        other = lax.ppermute(near_grad, "head", [(j, i) for i, j in up])
        add = other.astype(jnp.float32) + jnp.where(part == nhead - 1, total, 0.0)
    add = add.reshape(TOK, ngroup, 2, HEAD)
    dkey = dkey.at[rows - TOK :].add(add[:, :, 0].reshape(TOK, width_kv))
    dvalue = dvalue.at[rows - TOK :].add(add[:, :, 1].reshape(TOK, width_kv))
    return (
        attn[None], dquery[None],
        dkey.astype(jnp.bfloat16)[None], dvalue.astype(jnp.bfloat16)[None],
    )


def solution(mesh):
    spec = P("seq", "head", None)
    return jax.shard_map(
        shards,
        mesh=mesh,
        in_specs=(spec,) * 4 + (P(), P()),
        out_specs=(spec,) * 4,
        check_vma=False,
    )
```

```python
import functools
import math

import jax
import jax.numpy as jnp
from jax import lax
from jax.experimental import pallas as pl
from jax.experimental.pallas import tpu as pltpu
from jax.sharding import PartitionSpec as P

HEAD = 128
TOK = 128
MAXK = 3
DEAD = -1e30
CHUNKS = 1
SPLIT = 4


def attend(
    nb, nseq, query_group,
    meta,
    q_ref, g_ref, k_ref, v_ref, near_ref, tail_ref, *rest,
):
    out_ref, dq_ref, dk_ref, dv_ref, dnear_ref, dtail_ref, x_ref, pd_ref, far_ref = rest[-9:]
    f32, bf16 = jnp.float32, jnp.bfloat16
    scale = 1.0 / math.sqrt(HEAD)
    factor = scale * math.log2(math.e)
    zero = jnp.zeros((TOK, HEAD), bf16)
    causal = (
        lax.broadcasted_iota(jnp.int32, (TOK, TOK), 0)
        <= lax.broadcasted_iota(jnp.int32, (TOK, TOK), 1)
    )
    bias = jnp.where(causal, 0.0, DEAD).astype(f32)
    bias = jnp.concatenate([bias] * SPLIT, axis=1)
    prev_is_tail = meta[3 * nb] > 0
    prev_slot = pl.multiple_of(meta[3 * nb + 1] * TOK, TOK)
    dtail_ref[...] = jnp.zeros_like(dtail_ref)
    dnear_ref[...] = jnp.zeros_like(dnear_ref)

    for r in range(nb):
        rows = slice(r * TOK, (r + 1) * TOK)
        live = [None, meta[3 * r] > 0, meta[3 * r + 1] > 0]
        slot = pl.multiple_of(meta[3 * r + 2] * TOK, TOK)
        kv = [(k_ref[rows, :], v_ref[rows, :])]
        if r:
            before = slice((r - 1) * TOK, r * TOK)
            kv.append((k_ref[before, :], v_ref[before, :]))
        else:
            tail = tail_ref[pl.ds(prev_slot, TOK), :]
            pick = jnp.where(prev_is_tail, tail.astype(f32), near_ref[...].astype(f32)).astype(bf16)
            kv.append((pick[:, :HEAD], pick[:, HEAD:]))
        tail = tail_ref[pl.ds(slot, TOK), :]
        kv.append((tail[:, :HEAD], tail[:, HEAD:]))
        a = jnp.concatenate(
            [
                part
                for k, v in kv
                for part in (
                    jnp.concatenate([k, zero], axis=1),
                    jnp.concatenate([zero, v], axis=1),
                )
            ],
            axis=0,
        )
        b = jnp.concatenate(
            [
                jnp.concatenate(
                    [part for k, v in kv for part in (v.T, zero)], axis=1
                ),
                jnp.concatenate(
                    [part for k, v in kv for part in (zero, k.T)], axis=1
                ),
            ],
            axis=0,
        )
        for c in range(query_group // SPLIT):
            span = SPLIT * TOK
            at = slice(c * span, (c + 1) * span)
            for h in range(SPLIT):
                lanes = slice((c * SPLIT + h) * HEAD, (c * SPLIT + h + 1) * HEAD)
                there = slice((c * SPLIT + h) * TOK, (c * SPLIT + h + 1) * TOK)
                x_ref[there, :HEAD] = q_ref[rows, lanes]
                x_ref[there, HEAD:] = g_ref[rows, lanes]
            st = lax.dot_general(
                a, x_ref[at, :], (((1,), (1,)), ((), ())), preferred_element_type=f32
            )
            s = [st[2 * j * TOK : (2 * j + 1) * TOK] for j in range(MAXK)]
            dp = [st[(2 * j + 1) * TOK : (2 * j + 2) * TOK] for j in range(MAXK)]
            s[0] = s[0] + bias
            tops = [jnp.max(x, axis=0, keepdims=True) for x in s]
            top = tops[0]
            for j in (1, 2):
                top = jnp.maximum(top, jnp.where(live[j], tops[j], DEAD))
            p = []
            for j in range(MAXK):
                base = top if j == 0 else jnp.where(live[j], top, -DEAD)
                p.append(jnp.exp2((s[j] - base) * factor))
            total = sum(jnp.sum(x, axis=0, keepdims=True) for x in p)
            inv = 1.0 / total
            delta = sum(jnp.sum(x * y, axis=0, keepdims=True) for x, y in zip(p, dp)) * inv
            for j in range(MAXK):
                prob = p[j] * inv
                pd_ref[2 * j * TOK : (2 * j + 1) * TOK, at] = prob.astype(bf16)
                pd_ref[(2 * j + 1) * TOK : (2 * j + 2) * TOK, at] = (
                    prob * (dp[j] - delta)
                ).astype(bf16)
            ot = jnp.dot(b, pd_ref[:, at], preferred_element_type=f32)
            for h in range(SPLIT):
                lanes = slice((c * SPLIT + h) * HEAD, (c * SPLIT + h + 1) * HEAD)
                piece = ot[:, h * TOK : (h + 1) * TOK]
                out_ref[rows, lanes] = piece[:HEAD].T.astype(bf16)
                dq_ref[rows, lanes] = (piece[HEAD:].T * scale).astype(bf16)
        dkv = jnp.dot(pd_ref[...], x_ref[...], preferred_element_type=f32)

        def grads(j):
            return (
                dkv[(2 * j + 1) * TOK : (2 * j + 2) * TOK, :HEAD] * scale,
                dkv[2 * j * TOK : (2 * j + 1) * TOK, HEAD:],
            )

        dk, dv = grads(0)
        dk_ref[rows, :] = dk
        dv_ref[rows, :] = dv
        dk, dv = grads(1)
        if r:
            dk_ref[before, :] += dk
            dv_ref[before, :] += dv
        else:
            far_ref[nb, :, :HEAD] = dk
            far_ref[nb, :, HEAD:] = dv
        dk, dv = grads(2)
        far_ref[r, :, :HEAD] = dk
        far_ref[r, :, HEAD:] = dv

    first = far_ref[nb]
    first_far = jnp.logical_and(prev_is_tail, meta[0] > 0)

    @pl.when(jnp.logical_not(prev_is_tail))
    def _():
        dnear_ref[...] = first.astype(bf16)

    @pl.when(first_far)
    def _():
        dtail_ref[pl.ds(prev_slot, TOK), :] = first.astype(bf16)

    for r in range(nb):
        @pl.when(meta[3 * r + 1] > 0)
        def _(r=r):
            mine = meta[3 * r + 2]
            sum_ = far_ref[r]
            same = jnp.logical_and(first_far, meta[3 * nb + 1] == mine)
            sum_ = sum_ + jnp.where(same, far_ref[nb], 0.0)
            for e in range(r):
                same = jnp.logical_and(meta[3 * e + 1] > 0, meta[3 * e + 2] == mine)
                sum_ = sum_ + jnp.where(same, far_ref[e], 0.0)
            dtail_ref[pl.ds(pl.multiple_of(mine * TOK, TOK), TOK), :] = sum_.astype(bf16)


def call(nb, nseq, width, first, groups, query_group, meta, q, g, k, v, near, tails, earlier):
    rows = nb * TOK
    wide = query_group * HEAD
    width_kv = k.shape[1]

    def at(i, meta):
        return (0, i)

    def global_at(i, meta):
        return (0, first + i)

    big = pl.BlockSpec((rows, wide), global_at)
    own = pl.BlockSpec((rows, HEAD), global_at)
    in_specs = [
        big, big, own, own,
        pl.BlockSpec((TOK, 2 * HEAD), at),
        pl.BlockSpec((nseq * TOK, 2 * HEAD), at),
    ]
    operands = [q, g, k, v, near, tails]
    aliases = {}
    for i, e in enumerate(earlier):
        aliases[1 + len(operands)] = i
        operands.append(e)
        in_specs.append(pl.BlockSpec(memory_space=pl.ANY))
    bf16, f32 = jnp.bfloat16, jnp.float32
    sds = jax.ShapeDtypeStruct
    flops = 2 * rows * wide * MAXK * TOK * 6 * groups
    return pl.pallas_call(
        functools.partial(attend, nb, nseq, query_group),
        out_shape=(
            sds((rows, width), bf16), sds((rows, width), bf16),
            sds((rows, width_kv), f32), sds((rows, width_kv), f32),
            sds((TOK, groups * 2 * HEAD), bf16),
            sds((nseq * TOK, groups * 2 * HEAD), bf16),
        ),
        grid_spec=pltpu.PrefetchScalarGridSpec(
            num_scalar_prefetch=1,
            grid=(groups,),
            in_specs=in_specs,
            out_specs=[
                big, big, own, own,
                pl.BlockSpec((TOK, 2 * HEAD), at),
                pl.BlockSpec((nseq * TOK, 2 * HEAD), at),
            ],
            scratch_shapes=[
                pltpu.VMEM((query_group * TOK, 2 * HEAD), bf16),
                pltpu.VMEM((2 * MAXK * TOK, query_group * TOK), bf16),
                pltpu.VMEM((nb + 1, TOK, 2 * HEAD), f32),
            ],
        ),
        input_output_aliases=aliases,
        compiler_params=pltpu.CompilerParams(
            dimension_semantics=("arbitrary",), vmem_limit_bytes=48 * 1024 * 1024
        ),
        cost_estimate=pl.CostEstimate(
            flops=flops, bytes_accessed=4 * 2 * rows * wide * groups, transcendentals=0
        ),
        name="attend",
    )(meta, *operands)


PIECES = 4


def ring_place(n):
    across = n // 8
    me = lax.axis_index("seq")
    x, z = me // 2 % across, me // (2 * across)
    place = (x * 4 + z + (x % 2) * (3 - 2 * z)) * 2 + me % 2

    def index(p):
        p = (p + n) % n
        x, z = p // 8, p // 2 % 4
        z = z + (x % 2) * (3 - 2 * z)
        return z * (2 * across) + x * 2 + p % 2

    return me, place, index


def greet(left, right):
    barrier = pltpu.get_barrier_semaphore()
    for neighbour in (left, right):
        pl.semaphore_signal(
            barrier, inc=1, device_id={"seq": neighbour}, device_id_type=pl.DeviceIdType.MESH
        )
    pl.semaphore_wait(barrier, 2)


LANES = [(way, piece) for piece in range(PIECES) for way in range(2)]


def gather_ring(n, half, tail_ref, out_ref, send_sem, recv_sem, own_sem):
    me, place, index = ring_place(n)
    right, left = index(place + 1), index(place - 1)
    size = TOK // PIECES
    greet(left, right)

    def window(t, way, piece):
        owner = index(place - t) if way == 0 else index(place + t)
        start = pl.multiple_of(owner * TOK + piece * size, size)
        return out_ref.at[pl.ds(start, size), pl.ds(way * half, half)]

    def copy(t, sem, way, piece, src=None):
        there = window(t, way, piece)
        return pltpu.make_async_remote_copy(
            src_ref=there if src is None else src,
            dst_ref=there,
            send_sem=send_sem.at[way, piece, sem],
            recv_sem=recv_sem.at[way, piece, sem],
            device_id={"seq": right if way == 0 else left},
            device_id_type=pl.DeviceIdType.MESH,
        )

    for way, piece in LANES:
        src = tail_ref.at[pl.ds(piece * size, size), pl.ds(way * half, half)]
        copy(0, 0, way, piece, src).start()
    own = pltpu.make_async_copy(
        tail_ref, out_ref.at[pl.ds(pl.multiple_of(me * TOK, TOK), TOK), :], own_sem
    )
    own.start()

    def step(t, carry):
        for way, piece in LANES:
            copy(t, t - 1, way, piece).wait_recv()
            copy(t, t, way, piece).start()
        return carry

    lax.fori_loop(1, n - 1, step, 0)
    for way, piece in LANES:
        copy(n - 1, n - 2, way, piece).wait_recv()
    own.wait()

    def finish(t, carry):
        for way, piece in LANES:
            copy(t, t, way, piece).wait_send()
        return carry

    lax.fori_loop(0, n - 1, finish, 0)


def reduce_ring(n, half, term_ref, sum_ref, slots, send_sem, recv_sem):
    me, place, index = ring_place(n)
    right, left = index(place + 1), index(place - 1)
    size = TOK // PIECES
    greet(left, right)

    def term(t, way, piece):
        owner = index(place - 1 - t) if way == 0 else index(place + 1 + t)
        start = pl.multiple_of(owner * TOK + piece * size, size)
        return term_ref.at[pl.ds(start, size), pl.ds(way * half, half)]

    def slot(t, way, piece):
        return slots.at[t, way, pl.ds(piece * size, size), :]

    def copy(t, way, piece, src):
        return pltpu.make_async_remote_copy(
            src_ref=src,
            dst_ref=slot(t, way, piece),
            send_sem=send_sem.at[way, piece, t],
            recv_sem=recv_sem.at[way, piece, t],
            device_id={"seq": right if way == 0 else left},
            device_id_type=pl.DeviceIdType.MESH,
        )

    for way, piece in LANES:
        copy(0, way, piece, term(0, way, piece)).start()

    def total(t, way, piece):
        held = slot(t - 1, way, piece)
        copy(t - 1, way, piece, held).wait_recv()
        return held[...].astype(jnp.float32) + term(t, way, piece)[...].astype(jnp.float32)

    def step(t, carry):
        for way, piece in LANES:
            value = total(t, way, piece)
            held = slot(t - 1, way, piece)
            held[...] = value.astype(jnp.bfloat16)
            copy(t, way, piece, held).start()
        return carry

    lax.fori_loop(1, n - 1, step, 0)
    for way, piece in LANES:
        sum_ref[piece * size : (piece + 1) * size, way * half : (way + 1) * half] = total(
            n - 1, way, piece
        ).astype(jnp.bfloat16)

    def finish(t, carry):
        for way, piece in LANES:
            copy(t, way, piece, slot(t, way, piece)).wait_send()
        return carry

    lax.fori_loop(0, n - 1, finish, 0)


def gather(tail, n):
    half = tail.shape[1] // 2
    sems = pltpu.SemaphoreType.DMA((2, PIECES, n - 1))
    return pl.pallas_call(
        functools.partial(gather_ring, n, half),
        out_shape=jax.ShapeDtypeStruct((n * TOK, 2 * half), tail.dtype),
        in_specs=[pl.BlockSpec(memory_space=pl.ANY)],
        out_specs=pl.BlockSpec(memory_space=pl.ANY),
        scratch_shapes=[sems, sems, pltpu.SemaphoreType.DMA],
        compiler_params=pltpu.CompilerParams(collective_id=0, has_side_effects=True),
        name="gather_ring",
    )(tail)


def reduce_scatter(terms, n):
    half = terms.shape[1] // 2
    sems = pltpu.SemaphoreType.DMA((2, PIECES, n - 1))
    return pl.pallas_call(
        functools.partial(reduce_ring, n, half),
        out_shape=jax.ShapeDtypeStruct((TOK, 2 * half), terms.dtype),
        in_specs=[pl.BlockSpec(memory_space=pltpu.VMEM)],
        out_specs=pl.BlockSpec(memory_space=pltpu.VMEM),
        scratch_shapes=[pltpu.VMEM((n - 1, 2, TOK, half), terms.dtype), sems, sems],
        compiler_params=pltpu.CompilerParams(
            collective_id=1, has_side_effects=True, vmem_limit_bytes=48 * 1024 * 1024
        ),
        name="reduce_ring",
    )(terms)


def shards(query, key, value, output_gradient, kv_index, count):
    nseq, nhead = lax.axis_size("seq"), lax.axis_size("head")
    shard, part = lax.axis_index("seq"), lax.axis_index("head")
    rows, width = query.shape[1:]
    width_kv = key.shape[2]
    nb = rows // TOK
    ngroup = width_kv // HEAD
    query_group = width // width_kv
    blocks = nb * nhead
    row0 = shard * blocks + part * nb
    ids = lax.dynamic_slice_in_dim(kv_index, row0, nb, 0)
    n = lax.dynamic_slice_in_dim(count, row0, nb, 0)
    row = row0 + jnp.arange(nb, dtype=jnp.int32)
    prev = (n >= 2) & (ids[:, 1] == row - 1)
    strided = (n == 3) | ((n == 2) & ~prev)
    owner = jnp.where(n == 3, ids[:, 2], ids[:, 1]) // blocks
    owner = jnp.where(strided, owner, 0)
    per_row = jnp.stack([prev.astype(jnp.int32), strided.astype(jnp.int32), owner], axis=1)
    ends = jnp.stack([(part == 0).astype(jnp.int32), jnp.maximum(shard - 1, 0)])
    meta = jnp.concatenate([per_row.reshape(-1), ends]).astype(jnp.int32)

    q, g, k, v = query[0], output_gradient[0], key[0], value[0]
    last = jnp.stack(
        [k[rows - TOK :].reshape(TOK, ngroup, HEAD), v[rows - TOK :].reshape(TOK, ngroup, HEAD)],
        axis=2,
    ).reshape(TOK, 2 * width_kv)
    step = ngroup // CHUNKS
    cols = step * 2 * HEAD
    up = [(i, i + 1) for i in range(nhead - 1)]
    pair = [(0, 1), (1, 0)]
    if nhead == 2:
        near = lax.ppermute(last, "head", pair)
        tail = jnp.where(part == 1, last, near)
    else:
        near = lax.ppermute(last, "head", up)
        tail = lax.all_gather(last, "head", axis=0)[nhead - 1]
    gathered = [
        gather(tail[:, c * cols : (c + 1) * cols], nseq)
        for c in range(CHUNKS)
    ]
    earlier = ()
    tail_grads, near_grads = [], []
    for c in range(CHUNKS):
        *earlier, near_grad, tail_grad = call(
            nb, nseq, width, c * step, step, query_group, meta, q, g, k, v,
            near[:, c * cols : (c + 1) * cols], gathered[c], earlier,
        )
        near_grads.append(near_grad)
        tail_grads.append(reduce_scatter(tail_grad, nseq))
    attn, dquery, dkey, dvalue = earlier
    near_grad = jnp.concatenate(near_grads, axis=1)
    tail_grad = jnp.concatenate(tail_grads, axis=1)
    if nhead == 2:
        other = lax.ppermute(jnp.where(part == 0, tail_grad, near_grad), "head", pair)
        add = other.astype(jnp.float32) + jnp.where(part == 1, tail_grad.astype(jnp.float32), 0.0)
    else:
        total = lax.psum(tail_grad, "head").astype(jnp.float32)
        other = lax.ppermute(near_grad, "head", [(j, i) for i, j in up])
        add = other.astype(jnp.float32) + jnp.where(part == nhead - 1, total, 0.0)
    add = add.reshape(TOK, ngroup, 2, HEAD)
    dkey = dkey.at[rows - TOK :].add(add[:, :, 0].reshape(TOK, width_kv))
    dvalue = dvalue.at[rows - TOK :].add(add[:, :, 1].reshape(TOK, width_kv))
    return (
        attn[None], dquery[None],
        dkey.astype(jnp.bfloat16)[None], dvalue.astype(jnp.bfloat16)[None],
    )


def solution(mesh):
    spec = P("seq", "head", None)
    return jax.shard_map(
        shards,
        mesh=mesh,
        in_specs=(spec,) * 4 + (P(), P()),
        out_specs=(spec,) * 4,
        check_vma=False,
    )
```
